256 devices in a mesh: rep: 16 (over y_lo, z), fsdp: 16 (over x, y_hi, core).
Axes of the slice: x: 4, y: 4 (y_hi: 2, y_lo: 2; y = y_hi * 2 + y_lo), z: 8, core: 2. Of those that a mesh axis runs over, the one named last changes fastest.
Arguments:
- step_index: int32 [1], replicated, may hold values from 1 to 60
- tokens: bfloat16 [16, 2048, 5120], P('rep', 'fsdp'), may hold values from -120 to 120
- cotangent: bfloat16 [16, 2048, 2560], P('rep', 'fsdp'), may hold values from -0.3125 to 0.3125
- weight: float32 [16, 5120, 2560], P('rep', 'fsdp'), may hold values from -6 to 6
- weight_m: bfloat16 [16, 5120, 2560], P('rep', 'fsdp'), may hold values from -0.21875 to 0.21875
- weight_v: bfloat16 [16, 5120, 2560], P('rep', 'fsdp'), may hold values from 9.715557e-06 to 9.727478e-05
- gain: float32 [16, 5120], P('rep', 'fsdp'), may hold values from 0.5 to 1.5
- gain_m: float32 [16, 5120], P('rep', 'fsdp'), may hold values from -6 to 6
- gain_v: float32 [16, 5120], P('rep', 'fsdp'), may hold values from 0.05 to 0.5
Outputs:
- new_weight: float32 [16, 5120, 2560], P('rep', 'fsdp')
- new_gain: float32 [16, 5120], P('rep', 'fsdp')
The draws below stay inside these ranges and needn't reach their ends.
All inputs are finite; a program needn't handle non-finite values.
Results may differ from the reference program's by a relative error of at most 0.0003.
Values may be sent and summed in bfloat16 or wider, within the bound.
No kernel may reach another device: no remote copies, remote signals or barrier semaphores. Data moves between devices by JAX's collectives and lax.ppermute only.
A program may use at most 128 MiB of HBM per device.

```python
import math
import jax
import jax.numpy as jnp
from jax import lax

D = 5120
TOK_DEV = 128
HQ = 2560
TOK_REP = 2048
N_REP = 16
N_FSDP = 16


def draw_tokens(key, part):
    key = jax.random.fold_in(key, 11)
    key_base, key_rows, key_cols = jax.random.split(key, 3)
    shape = (N_REP, TOK_DEV * N_FSDP, D)
    base = jnp.clip(jax.random.normal(key_base, shape, jnp.float32), -4.0, 4.0)
    ramp = 3.0
    row_scale = 10.0 ** jax.random.uniform(key_rows, (N_REP, TOK_DEV * N_FSDP, 1), jnp.float32)
    position = jnp.arange(D, dtype=jnp.float32) / D
    col_scale = ramp ** position[None, None, :] * 10.0 ** jax.random.uniform(key_cols, (1, 1, D), jnp.float32)
    return (0.1 * base * row_scale * col_scale).astype(jnp.bfloat16)


def block_levels(own_key, extent, cuts, smallest, high):
    loudness, own = 1.0, jax.random.fold_in(own_key, 6)
    for dim, parts in cuts:
        draws = jnp.exp(jax.random.uniform(jax.random.fold_in(own, dim), (parts,), jnp.float32, smallest / len(cuts), high / len(cuts)))
        loudness = loudness * jnp.repeat(draws, extent[dim] // parts).reshape([-1 if axis == dim else 1 for axis in range(len(extent))])
    return loudness


def normal_values(stream_key, extent, width, limit, shards=(), kind=jnp.bfloat16):
    array = jax.random.normal(stream_key, extent, jnp.float32) * width
    if len(shards) > 0:
        array = block_levels(stream_key, extent, shards, -0.22, 0.18) * array
    return jnp.clip(array, min=-limit, max=limit).astype(kind)


def setup_inputs(seed: int = 0) -> dict:
    key_of = jax.random.split(jax.random.key(seed), 10)
    return {
        "step_index": jax.random.randint(key_of[0], (1,), 1, 61).astype(jnp.int32),
        "tokens": draw_tokens(jax.random.fold_in(key_of[9], 71), 0),
        "cotangent": normal_values(key_of[2], (N_REP, TOK_REP, HQ), (1.0 / TOK_REP ** 0.5), 0.3125, ((0, 16), (1, 16))),
        "weight": normal_values(key_of[3], (N_REP, D, HQ), 1.0, 6.0, ((0, 16), (1, 16)), jnp.float32),
        "weight_m": normal_values(key_of[4], (N_REP, D, HQ), (1.0 / D ** 0.5), 0.21875, ((0, 16), (1, 16))),
        "weight_v": jnp.clip(jnp.exp(math.log(9.72747802734375e-05) - 2.3038113 * jax.random.uniform(key_of[5], (N_REP, D, HQ), jnp.float32) ** block_levels(key_of[5], (N_REP, D, HQ), ((0, 16), (1, 16)), -0.2, 0.2)), 9.715557098388672e-06, 9.72747802734375e-05).astype(jnp.bfloat16),
        "gain": jnp.clip(1.0 + 0.1 * jax.random.normal(key_of[6], (N_REP, D), jnp.float32), 0.5, 1.5),
        "gain_m": normal_values(key_of[7], (N_REP, D), 0.5, 6.0, ((0, 16), (1, 16)), jnp.float32),
        "gain_v": jnp.clip(jnp.exp(math.log(0.5) - 2.3025851 * jax.random.uniform(key_of[8], (N_REP, D), jnp.float32) ** block_levels(key_of[8], (N_REP, D), ((0, 16), (1, 16)), -0.2, 0.2)), 0.05, 0.5),
    }


BETA_ONE = 0.9
BETA_TWO = 0.95
ADAM_EPS = 1e-08
RATE = 0.05
DECAY = 0.1
NORM_EPS = 1e-05

def adam_direction(param, first, second, grad, step, decay):
    moment_one = BETA_ONE * first.astype(jnp.float32) + (1.0 - BETA_ONE) * grad
    moment_two = BETA_TWO * second.astype(jnp.float32) + (1.0 - BETA_TWO) * grad * grad
    step_float = step.astype(jnp.float32)
    first_hat = moment_one / (1.0 - jnp.power(jnp.float32(BETA_ONE), step_float))
    second_hat = moment_two / (1.0 - jnp.power(jnp.float32(BETA_TWO), step_float))
    return first_hat / (jnp.sqrt(second_hat) + ADAM_EPS) + decay * param

def replica_step(operands, step):
    inputs, output_grad, own_weight, far_weight, first_w, second_w, own_gain, far_gain, first_g, second_g = operands
    wide = inputs.astype(jnp.float32)
    inverse_rms = lax.rsqrt(lax.optimization_barrier(jnp.mean(wide * wide, axis=1, keepdims=True)) + NORM_EPS)
    normed = wide * inverse_rms
    hidden = (normed * own_gain[None, :]).astype(jnp.bfloat16)
    weight_half = own_weight.astype(jnp.bfloat16)
    weight_grad = lax.dot_general(hidden, output_grad, (((0,), (0,)), ((), ())), preferred_element_type=jnp.float32) / math.sqrt(D)
    normed_grad = lax.dot_general(output_grad, weight_half, (((1,), (1,)), ((), ())), preferred_element_type=jnp.float32) / math.sqrt(D)
    gain_grad = lax.optimization_barrier(jnp.sum(normed * normed_grad, axis=0))
    weight_move = adam_direction(own_weight, first_w, second_w, weight_grad, step, DECAY)
    gain_move = adam_direction(own_gain, first_g, second_g, gain_grad, step, 0.0)
    new_weight = (own_weight + far_weight) * 0.5 - RATE * weight_move
    new_gain = (own_gain + far_gain) * 0.5 - RATE * gain_move
    return (new_weight, new_gain)

def reference(step_index, tokens, cotangent, weight, weight_m, weight_v, gain, gain_m, gain_v):
    levels = N_REP.bit_length() - 1
    step = step_index[0]
    distance = jnp.left_shift(jnp.int32(1), (step % levels).astype(jnp.int32))
    far_weight = jnp.roll(weight, distance, axis=0)
    far_gain = jnp.roll(gain, distance, axis=0)
    new_weight, new_gain = lax.map(lambda operands: replica_step(operands, step), (tokens, cotangent, weight, far_weight, weight_m, weight_v, gain, far_gain, gain_m, gain_v))
    return (new_weight, new_gain)
```

```python
from functools import partial
import math

import jax
import jax.numpy as jnp
from jax import lax
from jax.experimental import pallas as pl
from jax.experimental.pallas import tpu as pltpu
from jax.sharding import Mesh, PartitionSpec as P

BETA_ONE = 0.9
BETA_TWO = 0.95
ADAM_EPS = 1e-08
RATE = 0.05
DECAY = 0.1
NORM_EPS = 1e-05

REP, NX, NY, NC = 16, 4, 2, 2
PEERS = NX * NY
TOK, D, HQ, ROWS = 128, 5120, 2560, 320
PAIR = NC * ROWS
CODE_MAX = 32767.0
TINY = 1e-30
AXES = ("rep", "x", "y", "core")
VMEM_LIMIT = 48 * 1024 * 1024


def call(body, cost, **kwargs):
    flops, moved = cost
    return pl.pallas_call(
        body,
        compiler_params=pltpu.CompilerParams(vmem_limit_bytes=VMEM_LIMIT),
        cost_estimate=pl.CostEstimate(flops=flops, bytes_accessed=moved, transcendentals=0),
        **kwargs,
    )


def code_kernel(weight_ref, code_ref, scale_ref):
    block = weight_ref[...]
    peak = jnp.maximum(jnp.max(jnp.abs(block), axis=0, keepdims=True), TINY)
    code_ref[...] = jnp.round(block * (CODE_MAX / peak)).astype(jnp.int32).astype(jnp.int16)
    scale_ref[...] = peak * (0.5 / CODE_MAX)


def code_weight(weight):
    wide = 512
    return call(
        code_kernel,
        (4 * ROWS * HQ, 6 * ROWS * HQ),
        grid=(HQ // wide,),
        in_specs=[pl.BlockSpec((ROWS, wide), lambda j: (0, j))],
        out_specs=[pl.BlockSpec((ROWS, wide), lambda j: (0, j)), pl.BlockSpec((1, wide), lambda j: (0, j))],
        out_shape=[
            jax.ShapeDtypeStruct((ROWS, HQ), jnp.int16),
            jax.ShapeDtypeStruct((1, HQ), jnp.float32),
        ],
    )(weight)


def token_kernel(tokens_ref, cotangent_ref, scaled_ref, cut_ref):
    wide = tokens_ref[...].astype(jnp.float32)
    inverse_rms = lax.rsqrt(jnp.mean(wide * wide, axis=1, keepdims=True) + NORM_EPS)
    scaled_ref[...] = (cotangent_ref[...].astype(jnp.float32) * inverse_rms).astype(jnp.bfloat16)
    for peer in range(PEERS):
        cut_ref[peer] = tokens_ref[:, peer * PAIR : (peer + 1) * PAIR]


def prepare_tokens(tokens, cotangent):
    rows = 32
    return call(
        token_kernel,
        (4 * TOK * D, 4 * TOK * (D + HQ)),
        grid=(TOK // rows,),
        in_specs=[pl.BlockSpec((rows, D), lambda i: (i, 0)), pl.BlockSpec((rows, HQ), lambda i: (i, 0))],
        out_specs=[pl.BlockSpec((rows, HQ), lambda i: (i, 0)), pl.BlockSpec((PEERS, rows, PAIR), lambda i: (0, i, 0))],
        out_shape=[
            jax.ShapeDtypeStruct((TOK, HQ), jnp.bfloat16),
            jax.ShapeDtypeStruct((PEERS, TOK, PAIR), jnp.bfloat16),
        ],
    )(tokens, cotangent)


def turn_kernel(order_ref, columns_ref, turned_ref):
    turned_ref[...] = columns_ref[0].T


def turn_columns(order, columns):
    return pl.pallas_call(
        turn_kernel,
        grid_spec=pltpu.PrefetchScalarGridSpec(
            num_scalar_prefetch=1,
            grid=(PEERS,),
            in_specs=[pl.BlockSpec((1, TOK, PAIR), lambda k, order: (order[k], 0, 0))],
            out_specs=pl.BlockSpec((PAIR, TOK), lambda k, order: (0, k)),
        ),
        out_shape=jax.ShapeDtypeStruct((PAIR, PEERS * TOK), jnp.bfloat16),
        compiler_params=pltpu.CompilerParams(vmem_limit_bytes=VMEM_LIMIT),
        cost_estimate=pl.CostEstimate(flops=0, bytes_accessed=4 * PAIR * PEERS * TOK, transcendentals=0),
    )(order, columns)


def product_kernel(core_ref, turned_ref, *refs):
    stacked = jnp.concatenate([ref[...] for ref in refs[:-1]], axis=0)
    refs[-1][...] = jnp.dot(turned_ref[...], stacked, preferred_element_type=jnp.float32)


def product(core, turned, parts):
    wide = 512
    return pl.pallas_call(
        product_kernel,
        grid_spec=pltpu.PrefetchScalarGridSpec(
            num_scalar_prefetch=1,
            grid=(HQ // wide,),
            in_specs=[pl.BlockSpec((ROWS, PEERS * TOK), lambda j, core: (core[0], 0))]
            + [pl.BlockSpec((part.shape[0], wide), lambda j, core: (0, j)) for part in parts],
            out_specs=pl.BlockSpec((ROWS, wide), lambda j, core: (0, j)),
        ),
        out_shape=jax.ShapeDtypeStruct((ROWS, HQ), jnp.float32),
        compiler_params=pltpu.CompilerParams(vmem_limit_bytes=VMEM_LIMIT),
        cost_estimate=pl.CostEstimate(
            flops=2 * ROWS * PEERS * TOK * HQ, bytes_accessed=2 * PEERS * TOK * HQ + 4 * ROWS * HQ, transcendentals=0
        ),
    )(core, turned, *parts)


def adam_direction(param, first, second, grad, hat_one, hat_two, decay):
    moment_one = BETA_ONE * first.astype(jnp.float32) + (1.0 - BETA_ONE) * grad
    moment_two = BETA_TWO * second.astype(jnp.float32) + (1.0 - BETA_TWO) * grad * grad
    return (moment_one * hat_one) / (jnp.sqrt(moment_two * hat_two) + ADAM_EPS) + decay * param


def update_kernel(
    hats_ref, own_ref, far_ref, weight_ref, m_ref, v_ref, code_ref, scale_ref, gain_ref, gain_m_ref, gain_v_ref, far_gain_ref,
    new_weight_ref, new_gain_ref, column_ref, partial_ref,
):
    step, steps = pl.program_id(0), pl.num_programs(0)
    rows = weight_ref.shape[0]
    here = pl.ds(pl.multiple_of(step * rows, rows), rows)

    @pl.when(step == 0)
    def _():
        column_ref[...] = jnp.broadcast_to(gain_ref[...], (128, ROWS)).T

    hat_one, hat_two = hats_ref[0], hats_ref[1]
    total = (own_ref[...] + far_ref[...]) * (1.0 / math.sqrt(D))
    weight = weight_ref[...]
    half = weight.astype(jnp.bfloat16).astype(jnp.float32)
    moved = half * total
    folded = moved[:, :128]
    for lane in range(128, HQ, 128):
        folded = folded + moved[:, lane : lane + 128]
    partial_ref[here, :] = folded
    grad = total * column_ref[here, :1]
    move = adam_direction(weight, m_ref[...], v_ref[...], grad, hat_one, hat_two, DECAY)
    far_half = code_ref[...].astype(jnp.int32).astype(jnp.float32) * scale_ref[...]
    new_weight_ref[...] = weight * 0.5 + far_half - RATE * move

    @pl.when(step == steps - 1)
    def _():
        gain = gain_ref[...]
        gain_grad = jnp.sum(partial_ref[...].T, axis=0, keepdims=True)
        gain_move = adam_direction(gain, gain_m_ref[...], gain_v_ref[...], gain_grad, hat_one, hat_two, 0.0)
        new_gain_ref[...] = (gain + far_gain_ref[...]) * 0.5 - RATE * gain_move


def update(hats, own, far, weight, weight_m, weight_v, code, scale, gain, gain_m, gain_v, far_gain):
    rows = 64
    tall = pl.BlockSpec((rows, HQ), lambda i: (i, 0))
    thin = pl.BlockSpec((1, ROWS), lambda i: (0, 0))
    return call(
        update_kernel,
        (40 * ROWS * HQ, 22 * ROWS * HQ),
        grid=(ROWS // rows,),
        in_specs=[pl.BlockSpec(memory_space=pltpu.SMEM)]
        + [tall] * 6
        + [pl.BlockSpec((1, HQ), lambda i: (0, 0))]
        + [thin] * 4,
        out_specs=[tall, thin],
        out_shape=[
            jax.ShapeDtypeStruct((ROWS, HQ), jnp.float32),
            jax.ShapeDtypeStruct((1, ROWS), jnp.float32),
        ],
        scratch_shapes=[pltpu.VMEM((ROWS, 128), jnp.float32), pltpu.VMEM((ROWS, 128), jnp.float32)],
    )(hats, own, far, weight, weight_m, weight_v, code, scale, gain, gain_m, gain_v, far_gain)


def travel(block, target):
    sizes = (REP, NX, NY, NC)
    route = []
    for source in range(REP * NX * NY * NC):
        rep, rest = divmod(source, NX * NY * NC)
        x, rest = divmod(rest, NY * NC)
        y, core = divmod(rest, NC)
        place = 0
        for index, size in zip(target(rep, x, y, core), sizes):
            place = place * size + index % size
        route.append((source, place))
    return lax.ppermute(block, AXES, route)


def along_x(block, hop):
    return travel(block, lambda rep, x, y, core: (rep, x + hop, y, core))


def along_rep(block, hop):
    return travel(block, lambda rep, x, y, core: (rep + hop, x, y, core))


def other_y(block):
    return travel(block, lambda rep, x, y, core: (rep, x, 1 - y, core))


def other_core(block):
    return travel(block, lambda rep, x, y, core: (rep, x, y, 1 - core))


def around_x(block):
    left, right = along_x(block, 1), along_x(block, -1)
    half = block.shape[0] // 2
    return left, right, along_x(left[:half], 1), along_x(right[half:], -1)


def exchange(hats, code, side, scaled, cut, weight, weight_m, weight_v, gain, gain_m, gain_v, distance):
    x, y, core = lax.axis_index("x"), lax.axis_index("y"), lax.axis_index("core")
    far_code = along_rep(code, distance)
    far_side = along_rep(side, distance)
    across = other_y(scaled)
    near = around_x(scaled)
    columns = lax.all_to_all(cut, ("x", "y"), split_axis=0, concat_axis=0, tiled=True)
    beyond = around_x(across)
    parts = (scaled, *near, across, *beyond)
    hops = jnp.array([0, -1, 1, 2], jnp.int32)
    places = (x + hops) % NX * NY
    order = jnp.concatenate([places + y, places + 1 - y]).astype(jnp.int32)
    turned = turn_columns(order, columns)
    core = core.astype(jnp.int32)[None]
    sent = product(1 - core, turned, parts)
    far = other_core(sent)
    own = product(core, turned, parts)
    return update(
        hats, own, far, weight, weight_m, weight_v, far_code, far_side[:, :HQ], gain, gain_m, gain_v, far_side[:, HQ:]
    )


def shards(step_index, tokens, cotangent, weight, weight_m, weight_v, gain, gain_m, gain_v):
    step = step_index[0]
    step_float = step.astype(jnp.float32)
    hats = 1.0 / (1.0 - jnp.power(jnp.array([BETA_ONE, BETA_TWO], jnp.float32), step_float))
    code, scale = code_weight(weight[0])
    side = jnp.concatenate([scale, gain], axis=1)
    scaled, cut = prepare_tokens(tokens[0], cotangent[0])
    levels = REP.bit_length() - 1
    branches = [partial(exchange, distance=2**bit) for bit in range(levels)]
    new_weight, new_gain = lax.switch(
        step % levels, branches, hats, code, side, scaled, cut, weight[0], weight_m[0], weight_v[0], gain, gain_m, gain_v
    )
    return new_weight[None], new_gain


def solution(mesh):
    inner = Mesh(mesh.devices.reshape(REP, NX, NY, NC), AXES)
    fsdp = ("x", "y", "core")
    tall, thin = P("rep", fsdp, None), P("rep", fsdp)
    in_specs = (P(), tall, tall, tall, tall, tall, thin, thin, thin)
    return jax.shard_map(shards, mesh=inner, in_specs=in_specs, out_specs=(tall, thin), check_vma=False)
```

```python
from functools import partial
import math

import jax
import jax.numpy as jnp
from jax import lax
from jax.experimental import pallas as pl
from jax.experimental.pallas import tpu as pltpu
from jax.sharding import Mesh, PartitionSpec as P

BETA_ONE = 0.9
BETA_TWO = 0.95
ADAM_EPS = 1e-08
RATE = 0.05
DECAY = 0.1
NORM_EPS = 1e-05

REP, NX, NY, NC = 16, 4, 2, 2
PEERS = NX * NY
TOK, D, HQ, ROWS = 128, 5120, 2560, 320
PAIR = NC * ROWS
CODE_MAX = 32767.0
TINY = 1e-30
AXES = ("rep", "x", "y", "core")
WHOLE_VMEM, PART_VMEM = 60 * 1024 * 1024, 12 * 1024 * 1024


def call(body, cost, vmem, **kwargs):
    flops, moved = cost
    return pl.pallas_call(
        body,
        compiler_params=pltpu.CompilerParams(vmem_limit_bytes=vmem),
        cost_estimate=pl.CostEstimate(flops=flops, bytes_accessed=moved, transcendentals=0),
        **kwargs,
    )


def code_kernel(weight_ref, code_ref, scale_ref):
    block = weight_ref[...]
    peak = jnp.maximum(jnp.max(jnp.abs(block), axis=0, keepdims=True), TINY)
    code_ref[...] = jnp.round(block * (CODE_MAX / peak)).astype(jnp.int32).astype(jnp.int16)
    scale_ref[...] = peak * (0.5 / CODE_MAX)


def code_weight(weight):
    wide = 512
    return call(
        code_kernel,
        (4 * ROWS * HQ, 6 * ROWS * HQ),
        WHOLE_VMEM,
        grid=(HQ // wide,),
        in_specs=[pl.BlockSpec((ROWS, wide), lambda j: (0, j))],
        out_specs=[pl.BlockSpec((ROWS, wide), lambda j: (0, j)), pl.BlockSpec((1, wide), lambda j: (0, j))],
        out_shape=[
            jax.ShapeDtypeStruct((ROWS, HQ), jnp.int16),
            jax.ShapeDtypeStruct((1, HQ), jnp.float32),
        ],
    )(weight)


def scale_kernel(tokens_ref, cotangent_ref, scaled_ref):
    wide = tokens_ref[...].astype(jnp.float32)
    inverse_rms = lax.rsqrt(jnp.mean(wide * wide, axis=1, keepdims=True) + NORM_EPS)
    scaled_ref[...] = (cotangent_ref[...].astype(jnp.float32) * inverse_rms).astype(jnp.bfloat16)


def scale_cotangent(tokens, cotangent):
    rows = 32
    return call(
        scale_kernel,
        (4 * TOK * D, 2 * TOK * (D + 2 * HQ)),
        WHOLE_VMEM,
        grid=(TOK // rows,),
        in_specs=[pl.BlockSpec((rows, D), lambda i: (i, 0)), pl.BlockSpec((rows, HQ), lambda i: (i, 0))],
        out_specs=pl.BlockSpec((rows, HQ), lambda i: (i, 0)),
        out_shape=jax.ShapeDtypeStruct((TOK, HQ), jnp.bfloat16),
    )(tokens, cotangent)


def turn_kernel(tokens_ref, turned_ref):
    turned_ref[0] = tokens_ref[...].T


def turn_tokens(tokens):
    return call(
        turn_kernel,
        (0, 4 * TOK * D),
        WHOLE_VMEM,
        grid=(PEERS,),
        in_specs=[pl.BlockSpec((TOK, PAIR), lambda i: (0, i))],
        out_specs=pl.BlockSpec((1, PAIR, TOK), lambda i: (i, 0, 0)),
        out_shape=jax.ShapeDtypeStruct((PEERS, PAIR, TOK), jnp.bfloat16),
    )(tokens)


def product_kernel(order_ref, turned_ref, *refs):
    parts, total_ref, stacked_ref = refs[:-2], refs[-2], refs[-1]

    @pl.when(pl.program_id(0) == 0)
    def _():
        rows = pl.ds(pl.multiple_of(order_ref[PEERS] * ROWS, ROWS), ROWS)
        for place in range(PEERS):
            stacked_ref[:, place * TOK : (place + 1) * TOK] = turned_ref[order_ref[place], rows, :]

    gathered = jnp.concatenate([ref[...] for ref in parts], axis=0)
    total_ref[...] = jnp.dot(stacked_ref[...], gathered, preferred_element_type=jnp.float32)


def product(order, turned, parts):
    wide = 512
    return call(
        product_kernel,
        (2 * ROWS * PEERS * TOK * HQ, 2 * PEERS * TOK * HQ + 4 * ROWS * HQ),
        PART_VMEM,
        grid=(HQ // wide,),
        in_specs=[pl.BlockSpec(memory_space=pltpu.SMEM), pl.BlockSpec((PEERS, PAIR, TOK), lambda j: (0, 0, 0))]
        + [pl.BlockSpec((part.shape[0], wide), lambda j: (0, j)) for part in parts],
        out_specs=pl.BlockSpec((ROWS, wide), lambda j: (0, j)),
        out_shape=jax.ShapeDtypeStruct((ROWS, HQ), jnp.float32),
        scratch_shapes=[pltpu.VMEM((ROWS, PEERS * TOK), jnp.bfloat16)],
    )(order, turned, *parts)


def adam_direction(param, first, second, grad, hat_one, hat_two, decay):
    moment_one = BETA_ONE * first.astype(jnp.float32) + (1.0 - BETA_ONE) * grad
    moment_two = BETA_TWO * second.astype(jnp.float32) + (1.0 - BETA_TWO) * grad * grad
    return (moment_one * hat_one) / (jnp.sqrt(moment_two * hat_two) + ADAM_EPS) + decay * param


def update_kernel(
    hats_ref, own_ref, far_ref, weight_ref, m_ref, v_ref, code_ref, side_ref, gain_ref, gain_m_ref, gain_v_ref,
    new_weight_ref, new_gain_ref, column_ref, partial_ref,
):
    step, steps = pl.program_id(0), pl.num_programs(0)
    rows = new_weight_ref.shape[0]

    @pl.when(step == 0)
    def _():
        column_ref[...] = jnp.broadcast_to(gain_ref[...], (128, ROWS)).T

    hat_one, hat_two = hats_ref[0], hats_ref[1]
    keep_one, keep_two = BETA_ONE * hat_one, BETA_TWO * hat_two
    take_one, take_two = (1.0 - BETA_ONE) * hat_one, (1.0 - BETA_TWO) * hat_two
    tall = 16

    def rows_at(index, carry):
        here = pl.ds(pl.multiple_of(index * tall, tall), tall)
        there = pl.ds(pl.multiple_of(step * rows + index * tall, tall), tall)
        factor = column_ref[there, :1] * (1.0 / math.sqrt(D))
        folded = jnp.zeros((tall, 128), jnp.float32)
        for lane in range(0, HQ, 128):
            lanes = pl.ds(lane, 128)
            total = own_ref[there, lanes] + far_ref[there, lanes]
            weight = weight_ref[there, lanes]
            folded = folded + weight.astype(jnp.bfloat16).astype(jnp.float32) * total
            grad = total * factor
            first = keep_one * m_ref[there, lanes].astype(jnp.float32) + take_one * grad
            second = keep_two * v_ref[there, lanes].astype(jnp.float32) + take_two * (grad * grad)
            inverse = lax.rsqrt(second)
            move = first * inverse * (2.0 - (second * inverse + ADAM_EPS) * inverse)
            far_half = code_ref[there, lanes].astype(jnp.int32).astype(jnp.float32) * side_ref[:, lanes]
            new_weight_ref[here, lanes] = weight * (0.5 - RATE * DECAY) + far_half - RATE * move
        partial_ref[there, :] = folded
        return carry

    lax.fori_loop(0, rows // tall, rows_at, 0)

    @pl.when(step == steps - 1)
    def _():
        gain = gain_ref[...]
        gain_grad = jnp.sum(partial_ref[...].T, axis=0, keepdims=True) * (1.0 / math.sqrt(D))
        gain_move = adam_direction(gain, gain_m_ref[...], gain_v_ref[...], gain_grad, hat_one, hat_two, 0.0)
        new_gain_ref[...] = (gain + side_ref[:, HQ:]) * 0.5 - RATE * gain_move


def update(hats, own, far, weight, weight_m, weight_v, code, side, gain, gain_m, gain_v):
    rows = 32
    tall = pl.BlockSpec((rows, HQ), lambda i: (i, 0))
    thin = pl.BlockSpec((1, ROWS), lambda i: (0, 0))
    return call(
        update_kernel,
        (40 * ROWS * HQ, 22 * ROWS * HQ),
        2 * PART_VMEM,
        grid=(ROWS // rows,),
        in_specs=[pl.BlockSpec(memory_space=pltpu.SMEM)]
        + [pl.BlockSpec((ROWS, HQ), lambda i: (0, 0), pipeline_mode=pl.Buffered(1))] * 6
        + [pl.BlockSpec((1, HQ + ROWS), lambda i: (0, 0))]
        + [thin] * 3,
        out_specs=[tall, thin],
        out_shape=[
            jax.ShapeDtypeStruct((ROWS, HQ), jnp.float32),
            jax.ShapeDtypeStruct((1, ROWS), jnp.float32),
        ],
        scratch_shapes=[pltpu.VMEM((ROWS, 128), jnp.float32), pltpu.VMEM((ROWS, 128), jnp.float32)],
    )(hats, own, far, weight, weight_m, weight_v, code, side, gain, gain_m, gain_v)


def travel(block, target):
    sizes = (REP, NX, NY, NC)
    route = []
    for source in range(REP * NX * NY * NC):
        rep, rest = divmod(source, NX * NY * NC)
        x, rest = divmod(rest, NY * NC)
        y, core = divmod(rest, NC)
        place = 0
        for index, size in zip(target(rep, x, y, core), sizes):
            place = place * size + index % size
        route.append((source, place))
    return lax.ppermute(block, AXES, route)


def along_x(block, hop):
    return travel(block, lambda rep, x, y, core: (rep, x + hop, y, core))


def along_rep(block, hop):
    return travel(block, lambda rep, x, y, core: (rep + hop, x, y, core))


def other_y(block):
    return travel(block, lambda rep, x, y, core: (rep, x, 1 - y, core))


def other_core(block):
    return travel(block, lambda rep, x, y, core: (rep, x, y, 1 - core))


def exchange(code, side, pair, turned, distance):
    left, right = along_x(pair, 1), along_x(pair, -1)
    beyond = along_x(left[:TOK], 1), along_x(right[TOK:], -1)
    columns = lax.all_to_all(turned, ("x", "y"), split_axis=0, concat_axis=0, tiled=True)
    return along_rep(code, distance), along_rep(side, distance), columns, pair, left, right, *beyond


def shards(step_index, tokens, cotangent, weight, weight_m, weight_v, gain, gain_m, gain_v):
    step = step_index[0]
    step_float = step.astype(jnp.float32)
    hats = 1.0 / (1.0 - jnp.power(jnp.array([BETA_ONE, BETA_TWO], jnp.float32), step_float))
    x, y, core = lax.axis_index("x"), lax.axis_index("y"), lax.axis_index("core")
    places = [(x + hop) % NX * NY + lane for hop in (0, -1, 1, 2) for lane in (y, 1 - y)]
    orders = [jnp.stack([*places, which]).astype(jnp.int32) for which in (core, 1 - core)]

    scaled = scale_cotangent(tokens[0], cotangent[0])
    pair = jnp.concatenate([scaled, other_y(scaled)], axis=0)
    code, scale = code_weight(weight[0])
    turned = turn_tokens(tokens[0])
    side = jnp.concatenate([scale, gain], axis=1)
    side, hats, own_order, sent_order = lax.optimization_barrier((side, hats, *orders))
    levels = REP.bit_length() - 1
    branches = [partial(exchange, distance=2**bit) for bit in range(levels)]
    far_code, far_side, columns, *parts = lax.switch(step % levels, branches, code, side, pair, turned)

    sent = product(sent_order, columns, parts)
    far = other_core(sent)
    own = product(own_order, columns, parts)
    new_weight, new_gain = update(
        hats, own, far, weight[0], weight_m[0], weight_v[0], far_code, far_side, gain, gain_m, gain_v
    )
    return new_weight[None], new_gain


def solution(mesh):
    inner = Mesh(mesh.devices.reshape(REP, NX, NY, NC), AXES)
    fsdp = ("x", "y", "core")
    tall, thin = P("rep", fsdp, None), P("rep", fsdp)
    in_specs = (P(), tall, tall, tall, tall, tall, thin, thin, thin)
    return jax.shard_map(shards, mesh=inner, in_specs=in_specs, out_specs=(tall, thin), check_vma=False)
```

```python
from functools import partial
import math

import jax
import jax.numpy as jnp
from jax import lax
from jax.experimental import pallas as pl
from jax.experimental.pallas import tpu as pltpu
from jax.sharding import Mesh, PartitionSpec as P

BETA_ONE = 0.9
BETA_TWO = 0.95
ADAM_EPS = 1e-08
RATE = 0.05
DECAY = 0.1
NORM_EPS = 1e-05

REP, NX, NY, NC = 16, 4, 2, 2
PEERS = NX * NY
TOK, D, HQ, ROWS = 128, 5120, 2560, 320
PAIR = NC * ROWS
PIECES = 10
CODE_MAX = 32767.0
TINY = 1e-30
AXES = ("rep", "x", "y", "core")
WHOLE_VMEM, PART_VMEM = 62 * 1024 * 1024, 16 * 1024 * 1024


def call(body, cost, vmem, **kwargs):
    flops, moved = cost
    return pl.pallas_call(
        body,
        compiler_params=pltpu.CompilerParams(vmem_limit_bytes=vmem),
        cost_estimate=pl.CostEstimate(flops=flops, bytes_accessed=moved, transcendentals=0),
        **kwargs,
    )


def code_kernel(weight_ref, gain_ref, code_ref, scale_ref, column_ref):
    block = weight_ref[...]
    peak = jnp.maximum(jnp.max(jnp.abs(block), axis=0, keepdims=True), TINY)
    code_ref[...] = jnp.round(block * (CODE_MAX / peak)).astype(jnp.int32).astype(jnp.int16)
    scale_ref[...] = peak * (0.5 / CODE_MAX)

    @pl.when(pl.program_id(0) == 0)
    def _():
        column_ref[...] = jnp.broadcast_to(gain_ref[...] * (1.0 / math.sqrt(D)), (128, ROWS)).T


def code_weight(weight, gain):
    wide = 512
    return call(
        code_kernel,
        (4 * ROWS * HQ, 6 * ROWS * HQ),
        WHOLE_VMEM,
        grid=(HQ // wide,),
        in_specs=[pl.BlockSpec((ROWS, wide), lambda j: (0, j)), pl.BlockSpec((1, ROWS), lambda j: (0, 0))],
        out_specs=[
            pl.BlockSpec((ROWS, wide), lambda j: (0, j)),
            pl.BlockSpec((1, wide), lambda j: (0, j)),
            pl.BlockSpec((ROWS, 128), lambda j: (0, 0)),
        ],
        out_shape=[
            jax.ShapeDtypeStruct((ROWS, HQ), jnp.int16),
            jax.ShapeDtypeStruct((1, HQ), jnp.float32),
            jax.ShapeDtypeStruct((ROWS, 128), jnp.float32),
        ],
    )(weight, gain)


def scale_kernel(tokens_ref, cotangent_ref, scaled_ref):
    wide = tokens_ref[...].astype(jnp.float32)
    inverse_rms = lax.rsqrt(jnp.mean(wide * wide, axis=1, keepdims=True) + NORM_EPS)
    scaled_ref[...] = (cotangent_ref[...].astype(jnp.float32) * inverse_rms).astype(jnp.bfloat16)


def scale_cotangent(tokens, cotangent):
    rows = 32
    return call(
        scale_kernel,
        (4 * TOK * D, 2 * TOK * (D + 2 * HQ)),
        WHOLE_VMEM,
        grid=(TOK // rows,),
        in_specs=[pl.BlockSpec((rows, D), lambda i: (i, 0)), pl.BlockSpec((rows, HQ), lambda i: (i, 0))],
        out_specs=pl.BlockSpec((rows, HQ), lambda i: (i, 0)),
        out_shape=jax.ShapeDtypeStruct((TOK, HQ), jnp.bfloat16),
    )(tokens, cotangent)


def turn_kernel(tokens_ref, turned_ref):
    turned_ref[0] = tokens_ref[...].T


def turn_tokens(tokens):
    return call(
        turn_kernel,
        (0, 4 * TOK * D),
        WHOLE_VMEM,
        grid=(PEERS,),
        in_specs=[pl.BlockSpec((TOK, PAIR), lambda i: (0, i))],
        out_specs=pl.BlockSpec((1, PAIR, TOK), lambda i: (i, 0, 0)),
        out_shape=jax.ShapeDtypeStruct((PEERS, PAIR, TOK), jnp.bfloat16),
    )(tokens)


def product_kernel(leaves, step, order_ref, turned_ref, *refs):
    parts, total_ref, stacked_ref = refs[:PEERS], refs[PEERS], refs[PEERS + 1]
    kept_ref, sem = refs[PEERS + 2 :] if leaves else (total_ref, None)
    rows = pl.ds(pl.multiple_of(order_ref[PEERS] * ROWS, ROWS), ROWS)
    for place in range(PEERS):
        stacked_ref[:, place * TOK : (place + 1) * TOK] = turned_ref[order_ref[place], rows, :]

    def lanes_of(index):
        return pl.ds(pl.multiple_of(index * step, step), step)

    def leaving(index):
        return pltpu.make_async_copy(kept_ref.at[:, lanes_of(index)], total_ref.at[:, lanes_of(index)], sem.at[index])

    def columns_at(index, carry):
        gathered = jnp.concatenate([ref[:, lanes_of(index)] for ref in parts], axis=0)
        kept_ref[:, lanes_of(index)] = jnp.dot(stacked_ref[...], gathered, preferred_element_type=jnp.float32)
        if leaves:
            leaving(index).start()
        return carry

    lax.fori_loop(0, HQ // step, columns_at, 0)
    if leaves:
        for index in range(HQ // step):
            leaving(index).wait()


def product(order, turned, parts, leaves):
    vmem = pl.BlockSpec(memory_space=pltpu.VMEM)
    step = 512 if leaves else 256
    kept = [pltpu.VMEM((ROWS, HQ), jnp.float32), pltpu.SemaphoreType.DMA((HQ // step,))] if leaves else []
    return call(
        partial(product_kernel, leaves, step),
        (2 * ROWS * PEERS * TOK * HQ, 2 * PEERS * TOK * HQ + 4 * ROWS * HQ),
        PART_VMEM,
        in_specs=[pl.BlockSpec(memory_space=pltpu.SMEM)] + [vmem] * (1 + len(parts)),
        out_specs=pl.BlockSpec(memory_space=pl.ANY) if leaves else vmem,
        out_shape=jax.ShapeDtypeStruct((ROWS, HQ), jnp.float32),
        scratch_shapes=[pltpu.VMEM((ROWS, PEERS * TOK), jnp.bfloat16)] + kept,
    )(order, turned, *parts)


def adam_direction(param, first, second, grad, hat_one, hat_two, decay):
    moment_one = BETA_ONE * first.astype(jnp.float32) + (1.0 - BETA_ONE) * grad
    moment_two = BETA_TWO * second.astype(jnp.float32) + (1.0 - BETA_TWO) * grad * grad
    return (moment_one * hat_one) / (jnp.sqrt(moment_two * hat_two) + ADAM_EPS) + decay * param


def piece_rows(piece):
    return pl.ds(piece * (ROWS // PIECES), ROWS // PIECES)


def piece_copies(source, target, sem):
    return [
        pltpu.make_async_copy(source.at[piece_rows(piece)], target.at[piece_rows(piece)], sem.at[piece])
        for piece in range(PIECES)
    ]


def by_pieces(arriving, leaving, rows_at):
    tall, chunk = 16, ROWS // PIECES
    for copies in arriving:
        for copy in copies:
            copy.start()
    for piece in range(PIECES):
        for copies in arriving:
            copies[piece].wait()
        lax.fori_loop(
            piece * chunk // tall,
            (piece + 1) * chunk // tall,
            lambda index, carry: rows_at(pl.ds(pl.multiple_of(index * tall, tall), tall), carry),
            0,
        )
        leaving[piece].start()


def update_kernel(
    mixed, hats_ref, own_ref, far_ref, weight_ref, m_ref, v_ref, column_ref, gain_ref, gain_m_ref, gain_v_ref, *refs
):
    partner = refs[:2] if mixed else ()
    new_weight_ref, new_gain_ref, partial_ref, ready_ref, sent_sem = refs[len(partner) :]
    hat_one, hat_two = hats_ref[0], hats_ref[1]
    keep_one, keep_two = BETA_ONE * hat_one, BETA_TWO * hat_two
    take_one, take_two = (1.0 - BETA_ONE) * hat_one, (1.0 - BETA_TWO) * hat_two

    def rows_at(here, carry):
        factor = column_ref[here, :1]
        folded = jnp.zeros((here.size, 128), jnp.float32)
        for lane in range(0, HQ, 128):
            lanes = pl.ds(lane, 128)
            total = own_ref[here, lanes] + far_ref[here, lanes]
            weight = weight_ref[here, lanes]
            folded = folded + weight.astype(jnp.bfloat16).astype(jnp.float32) * total
            grad = total * factor
            first = keep_one * m_ref[here, lanes].astype(jnp.float32) + take_one * grad
            second = keep_two * v_ref[here, lanes].astype(jnp.float32) + take_two * (grad * grad)
            move = first / (second * lax.rsqrt(second) + ADAM_EPS)
            new_weight = weight * (0.5 - RATE * DECAY) - RATE * move
            if mixed:
                far_half = partner[0][here, lanes].astype(jnp.int32).astype(jnp.float32) * partner[1][:, lanes]
                new_weight = new_weight + far_half
            ready_ref[here, lanes] = new_weight
        partial_ref[here, :] = folded
        return carry

    leaving = piece_copies(ready_ref, new_weight_ref, sent_sem)
    by_pieces([], leaving, rows_at)
    gain = gain_ref[...]
    gain_grad = jnp.sum(partial_ref[...].T, axis=0, keepdims=True) * (1.0 / math.sqrt(D))
    gain_move = adam_direction(gain, gain_m_ref[...], gain_v_ref[...], gain_grad, hat_one, hat_two, 0.0)
    new_gain = gain * 0.5 - RATE * gain_move
    if mixed:
        new_gain = new_gain + partner[1][:, HQ:] * 0.5
    new_gain_ref[...] = new_gain
    for copy in leaving:
        copy.wait()


def update(hats, own, far, weight, weight_m, weight_v, column, gain, gain_m, gain_v, partner):
    vmem, anywhere = pl.BlockSpec(memory_space=pltpu.VMEM), pl.BlockSpec(memory_space=pl.ANY)
    return call(
        partial(update_kernel, len(partner) > 0),
        (0, 0),
        PART_VMEM,
        in_specs=[pl.BlockSpec(memory_space=pltpu.SMEM)] + [vmem] * (9 + len(partner)),
        out_specs=[anywhere, vmem],
        out_shape=[
            jax.ShapeDtypeStruct((ROWS, HQ), jnp.float32),
            jax.ShapeDtypeStruct((1, ROWS), jnp.float32),
        ],
        scratch_shapes=[
            pltpu.VMEM((ROWS, 128), jnp.float32),
            pltpu.VMEM((ROWS, HQ), jnp.float32),
            pltpu.SemaphoreType.DMA((PIECES,)),
        ],
    )(hats, own, far, weight, weight_m, weight_v, column, gain, gain_m, gain_v, *partner)


def mix_kernel(
    part_weight_ref, part_gain_ref, code_ref, side_ref, new_weight_ref, new_gain_ref,
    ready_ref, sent_sem, part_ref, part_sem, held_ref, held_sem,
):
    def rows_at(here, carry):
        far_half = held_ref[here, :].astype(jnp.int32).astype(jnp.float32) * side_ref[:, :HQ]
        ready_ref[here, :] = part_ref[here, :] + far_half
        return carry

    arriving = [piece_copies(part_weight_ref, part_ref, part_sem), piece_copies(code_ref, held_ref, held_sem)]
    leaving = piece_copies(ready_ref, new_weight_ref, sent_sem)
    by_pieces(arriving, leaving, rows_at)
    new_gain_ref[...] = part_gain_ref[...] + side_ref[:, HQ:] * 0.5
    for copy in leaving:
        copy.wait()


def mix(part_weight, part_gain, code, side):
    vmem, anywhere = pl.BlockSpec(memory_space=pltpu.VMEM), pl.BlockSpec(memory_space=pl.ANY)
    return call(
        mix_kernel,
        (0, 0),
        PART_VMEM,
        in_specs=[anywhere, vmem, anywhere, vmem],
        out_specs=[anywhere, vmem],
        out_shape=[
            jax.ShapeDtypeStruct((ROWS, HQ), jnp.float32),
            jax.ShapeDtypeStruct((1, ROWS), jnp.float32),
        ],
        scratch_shapes=[
            pltpu.VMEM((ROWS, HQ), jnp.float32),
            pltpu.SemaphoreType.DMA((PIECES,)),
            pltpu.VMEM((ROWS, HQ), jnp.float32),
            pltpu.SemaphoreType.DMA((PIECES,)),
            pltpu.VMEM((ROWS, HQ), jnp.int16),
            pltpu.SemaphoreType.DMA((PIECES,)),
        ],
    )(part_weight, part_gain, code, side)


def travel(block, target):
    sizes = (REP, NX, NY, NC)
    route = []
    for source in range(REP * NX * NY * NC):
        rep, rest = divmod(source, NX * NY * NC)
        x, rest = divmod(rest, NY * NC)
        y, core = divmod(rest, NC)
        place = 0
        for index, size in zip(target(rep, x, y, core), sizes):
            place = place * size + index % size
        route.append((source, place))
    return lax.ppermute(block, AXES, route)


def along_x(block, hop):
    return travel(block, lambda rep, x, y, core: (rep, x + hop, y, core))


def along_rep(block, hop):
    return travel(block, lambda rep, x, y, core: (rep + hop, x, y, core))


def other_y(block):
    return travel(block, lambda rep, x, y, core: (rep, x, 1 - y, core))


def other_core(block):
    return travel(block, lambda rep, x, y, core: (rep, x, y, 1 - core))


def finish(sent, order, columns, parts, hats, weight, weight_m, weight_v, column, gain, gain_m, gain_v, partner):
    far = other_core(sent)
    own = product(order, columns, parts, False)
    return tuple(update(hats, own, far, weight, weight_m, weight_v, column, gain, gain_m, gain_v, partner))


def nothing(*given):
    return jnp.zeros((ROWS, HQ), jnp.float32), jnp.zeros((1, ROWS), jnp.float32)


def exchange(
    step, code, side, scaled, across, left, right, turned, order, own_order, hats, weight, weight_m, weight_v,
    column, gain, gain_m, gain_v, distance,
):
    far_code, far_side = along_rep(code, distance), along_rep(side, distance)
    right_across, beyond = along_x(across, -1), along_x(left, 1)
    columns = lax.all_to_all(turned, ("x", "y"), split_axis=0, concat_axis=0, tiled=True)
    left_across = along_x(across, 1)
    right_across, beyond = lax.optimization_barrier((right_across, beyond))
    parts = scaled, across, left, right, right_across, beyond, left_across, along_x(right_across, -1)
    apart = distance in (2, 4)
    ended = lax.cond(
        step > 0, finish, nothing, product(order, columns, parts, True), own_order, columns, parts, hats,
        weight, weight_m, weight_v, column, gain, gain_m, gain_v, () if apart else (far_code, far_side),
    )
    return tuple(mix(*ended, far_code, far_side)) if apart else ended


def shards(step_index, tokens, cotangent, weight, weight_m, weight_v, gain, gain_m, gain_v):
    step = step_index[0]
    step_float = step.astype(jnp.float32)
    hats = 1.0 / (1.0 - jnp.power(jnp.array([BETA_ONE, BETA_TWO], jnp.float32), step_float))
    x, y, core = lax.axis_index("x"), lax.axis_index("y"), lax.axis_index("core")
    near = ((0, y), (0, 1 - y), (-1, y), (1, y), (1, 1 - y), (2, y), (-1, 1 - y), (2, 1 - y))
    places = [(x + hop) % NX * NY + lane for hop, lane in near]
    orders = [jnp.stack([*places, which]).astype(jnp.int32) for which in (1 - core, core)]

    scaled = scale_cotangent(tokens[0], cotangent[0])
    across, left, right = other_y(scaled), along_x(scaled, 1), along_x(scaled, -1)
    code, scale, column = code_weight(weight[0], gain)
    turned = turn_tokens(tokens[0])
    side = jnp.concatenate([scale, gain], axis=1)
    side, hats, order, own_order = lax.optimization_barrier((side, hats, *orders))
    levels = REP.bit_length() - 1
    branches = [partial(exchange, distance=2**bit) for bit in range(levels)]
    new_weight, new_gain = lax.switch(
        step % levels, branches, step, code, side, scaled, across, left, right, turned, order, own_order, hats,
        weight[0], weight_m[0], weight_v[0], column, gain, gain_m, gain_v,
    )
    return new_weight[None], new_gain


def solution(mesh):
    inner = Mesh(mesh.devices.reshape(REP, NX, NY, NC), AXES)
    fsdp = ("x", "y", "core")
    tall, thin = P("rep", fsdp, None), P("rep", fsdp)
    in_specs = (P(), tall, tall, tall, tall, tall, thin, thin, thin)
    return jax.shard_map(shards, mesh=inner, in_specs=in_specs, out_specs=(tall, thin), check_vma=False)
```

```python
from functools import partial
import math

import jax
import jax.numpy as jnp
from jax import lax
from jax.experimental import pallas as pl
from jax.experimental.pallas import tpu as pltpu
from jax.sharding import Mesh, PartitionSpec as P

BETA_ONE = 0.9
BETA_TWO = 0.95
ADAM_EPS = 1e-08
RATE = 0.05
DECAY = 0.1
NORM_EPS = 1e-05

REP, NX, NY, NC = 16, 4, 2, 2
PEERS = NX * NY
TOK, D, HQ, ROWS = 128, 5120, 2560, 320
PAIR = NC * ROWS
PIECES, SEGMENTS = 20, 5
AHEAD = 256
CODE_MAX = 32767.0
TINY = 1e-30
AXES = ("rep", "x", "y", "core")
WHOLE_VMEM, PART_VMEM = 62 * 1024 * 1024, 16 * 1024 * 1024


def call(body, cost, vmem, **kwargs):
    flops, moved = cost
    return pl.pallas_call(
        body,
        compiler_params=pltpu.CompilerParams(vmem_limit_bytes=vmem),
        cost_estimate=pl.CostEstimate(flops=flops, bytes_accessed=moved, transcendentals=0),
        **kwargs,
    )


def code_kernel(weight_ref, gain_ref, code_ref, head_ref, tail_ref, scale_ref, column_ref):
    block = weight_ref[...]
    peak = jnp.maximum(jnp.max(jnp.abs(block), axis=0, keepdims=True), TINY)
    code = jnp.round(block * (CODE_MAX / peak)).astype(jnp.int32).astype(jnp.int16)
    code_ref[...], head_ref[...], tail_ref[...] = code, code[:AHEAD], code[AHEAD:]
    scale_ref[...] = peak * (0.5 / CODE_MAX)

    @pl.when(pl.program_id(0) == 0)
    def _():
        column_ref[...] = jnp.broadcast_to(gain_ref[...] * (1.0 / math.sqrt(D)), (128, ROWS)).T


def code_weight(weight, gain):
    wide = 512
    return call(
        code_kernel,
        (4 * ROWS * HQ, 6 * ROWS * HQ),
        WHOLE_VMEM,
        grid=(HQ // wide,),
        in_specs=[pl.BlockSpec((ROWS, wide), lambda j: (0, j)), pl.BlockSpec((1, ROWS), lambda j: (0, 0))],
        out_specs=[
            pl.BlockSpec((ROWS, wide), lambda j: (0, j)),
            pl.BlockSpec((AHEAD, wide), lambda j: (0, j)),
            pl.BlockSpec((ROWS - AHEAD, wide), lambda j: (0, j)),
            pl.BlockSpec((1, wide), lambda j: (0, j)),
            pl.BlockSpec((ROWS, 128), lambda j: (0, 0)),
        ],
        out_shape=[
            jax.ShapeDtypeStruct((ROWS, HQ), jnp.int16),
            jax.ShapeDtypeStruct((AHEAD, HQ), jnp.int16),
            jax.ShapeDtypeStruct((ROWS - AHEAD, HQ), jnp.int16),
            jax.ShapeDtypeStruct((1, HQ), jnp.float32),
            jax.ShapeDtypeStruct((ROWS, 128), jnp.float32),
        ],
    )(weight, gain)


def scale_kernel(tokens_ref, cotangent_ref, scaled_ref):
    wide = tokens_ref[...].astype(jnp.float32)
    inverse_rms = lax.rsqrt(jnp.mean(wide * wide, axis=1, keepdims=True) + NORM_EPS)
    scaled_ref[...] = (cotangent_ref[...].astype(jnp.float32) * inverse_rms).astype(jnp.bfloat16)


def scale_cotangent(tokens, cotangent):
    rows = 32
    return call(
        scale_kernel,
        (4 * TOK * D, 2 * TOK * (D + 2 * HQ)),
        WHOLE_VMEM,
        grid=(TOK // rows,),
        in_specs=[pl.BlockSpec((rows, D), lambda i: (i, 0)), pl.BlockSpec((rows, HQ), lambda i: (i, 0))],
        out_specs=pl.BlockSpec((rows, HQ), lambda i: (i, 0)),
        out_shape=jax.ShapeDtypeStruct((TOK, HQ), jnp.bfloat16),
    )(tokens, cotangent)


def turn_kernel(tokens_ref, turned_ref):
    turned_ref[0] = tokens_ref[...].T


def turn_tokens(tokens):
    return call(
        turn_kernel,
        (0, 4 * TOK * D),
        WHOLE_VMEM,
        grid=(PEERS,),
        in_specs=[pl.BlockSpec((TOK, PAIR), lambda i: (0, i))],
        out_specs=pl.BlockSpec((1, PAIR, TOK), lambda i: (i, 0, 0)),
        out_shape=jax.ShapeDtypeStruct((PEERS, PAIR, TOK), jnp.bfloat16),
    )(tokens)


def product_kernel(leaves, step, order_ref, turned_ref, *refs):
    parts, total_ref, stacked_ref = refs[:PEERS], refs[PEERS], refs[PEERS + 1]
    kept_ref, sem = refs[PEERS + 2 :] if leaves else (total_ref, None)
    rows = pl.ds(pl.multiple_of(order_ref[PEERS] * ROWS, ROWS), ROWS)
    for place in range(PEERS):
        stacked_ref[:, place * TOK : (place + 1) * TOK] = turned_ref[order_ref[place], rows, :]

    def lanes_of(index):
        return pl.ds(pl.multiple_of(index * step, step), step)

    def leaving(index):
        return pltpu.make_async_copy(kept_ref.at[:, lanes_of(index)], total_ref.at[:, lanes_of(index)], sem.at[index])

    def columns_at(index, carry):
        gathered = jnp.concatenate([ref[:, lanes_of(index)] for ref in parts], axis=0)
        kept_ref[:, lanes_of(index)] = jnp.dot(stacked_ref[...], gathered, preferred_element_type=jnp.float32)
        if leaves:
            leaving(index).start()
        return carry

    lax.fori_loop(0, HQ // step, columns_at, 0)
    if leaves:
        for index in range(HQ // step):
            leaving(index).wait()


def product(order, turned, parts, leaves):
    vmem = pl.BlockSpec(memory_space=pltpu.VMEM)
    step = 512
    kept = [pltpu.VMEM((ROWS, HQ), jnp.float32), pltpu.SemaphoreType.DMA((HQ // step,))] if leaves else []
    return call(
        partial(product_kernel, leaves, step),
        (2 * ROWS * PEERS * TOK * HQ, 2 * PEERS * TOK * HQ + 4 * ROWS * HQ),
        PART_VMEM,
        in_specs=[pl.BlockSpec(memory_space=pltpu.SMEM)] + [vmem] * (1 + len(parts)),
        out_specs=pl.BlockSpec(memory_space=pl.ANY) if leaves else vmem,
        out_shape=jax.ShapeDtypeStruct((ROWS, HQ), jnp.float32),
        scratch_shapes=[pltpu.VMEM((ROWS, PEERS * TOK), jnp.bfloat16)] + kept,
    )(order, turned, *parts)


def adam_direction(param, first, second, grad, hat_one, hat_two, decay):
    moment_one = BETA_ONE * first.astype(jnp.float32) + (1.0 - BETA_ONE) * grad
    moment_two = BETA_TWO * second.astype(jnp.float32) + (1.0 - BETA_TWO) * grad * grad
    return (moment_one * hat_one) / (jnp.sqrt(moment_two * hat_two) + ADAM_EPS) + decay * param


def update_kernel(
    mixed, hats_ref, own_ref, far_ref, weight_ref, m_ref, v_ref, column_ref, gain_ref, gain_m_ref, gain_v_ref, *refs
):
    partner = refs[:2] if mixed else ()
    new_weight_ref, new_gain_ref, partial_ref, ready_ref, sent_sem = refs[len(partner) :]
    hat_one, hat_two = hats_ref[0], hats_ref[1]
    keep_one, keep_two = BETA_ONE * hat_one, BETA_TWO * hat_two
    take_one, take_two = (1.0 - BETA_ONE) * hat_one, (1.0 - BETA_TWO) * hat_two

    tall = ROWS // PIECES

    def rows_at(here):
        factor = column_ref[here, :1]
        folded = jnp.zeros((here.size, 128), jnp.float32)
        for lane in range(0, HQ, 128):
            lanes = pl.ds(lane, 128)
            total = own_ref[here, lanes] + far_ref[here, lanes]
            weight = weight_ref[here, lanes]
            folded = folded + weight.astype(jnp.bfloat16).astype(jnp.float32) * total
            grad = total * factor
            first = keep_one * m_ref[here, lanes].astype(jnp.float32) + take_one * grad
            second = keep_two * v_ref[here, lanes].astype(jnp.float32) + take_two * (grad * grad)
            move = first / (second * lax.rsqrt(second) + ADAM_EPS)
            new_weight = weight * (0.5 - RATE * DECAY) - RATE * move
            if mixed:
                far_half = partner[0][here, lanes].astype(jnp.int32).astype(jnp.float32) * partner[1][:, lanes]
                new_weight = new_weight + far_half
            ready_ref[here, lanes] = new_weight
        partial_ref[here, :] = folded

    def leaving(piece):
        rows = pl.ds(pl.multiple_of(piece * tall, tall), tall)
        return pltpu.make_async_copy(ready_ref.at[rows], new_weight_ref.at[rows], sent_sem.at[piece])

    def piece_at(piece, carry):
        rows_at(pl.ds(pl.multiple_of(piece * tall, tall), tall))
        leaving(piece).start()
        return carry

    lax.fori_loop(0, PIECES, piece_at, 0)
    gain = gain_ref[...]
    gain_grad = jnp.sum(partial_ref[...].T, axis=0, keepdims=True) * (1.0 / math.sqrt(D))
    gain_move = adam_direction(gain, gain_m_ref[...], gain_v_ref[...], gain_grad, hat_one, hat_two, 0.0)
    new_gain = gain * 0.5 - RATE * gain_move
    if mixed:
        new_gain = new_gain + partner[1][:, HQ:] * 0.5
    new_gain_ref[...] = new_gain
    for piece in range(PIECES):
        leaving(piece).wait()


def update(hats, own, far, weight, weight_m, weight_v, column, gain, gain_m, gain_v, partner):
    vmem, anywhere = pl.BlockSpec(memory_space=pltpu.VMEM), pl.BlockSpec(memory_space=pl.ANY)
    return call(
        partial(update_kernel, len(partner) > 0),
        (0, 0),
        PART_VMEM,
        in_specs=[pl.BlockSpec(memory_space=pltpu.SMEM)] + [vmem] * (9 + len(partner)),
        out_specs=[anywhere, vmem],
        out_shape=[
            jax.ShapeDtypeStruct((ROWS, HQ), jnp.float32),
            jax.ShapeDtypeStruct((1, ROWS), jnp.float32),
        ],
        scratch_shapes=[
            pltpu.VMEM((ROWS, 128), jnp.float32),
            pltpu.VMEM((ROWS, HQ), jnp.float32),
            pltpu.SemaphoreType.DMA((PIECES,)),
        ],
    )(hats, own, far, weight, weight_m, weight_v, column, gain, gain_m, gain_v, *partner)


def mix_kernel(part_weight_ref, part_gain_ref, side_ref, *refs):
    code_refs = refs[:-8]
    new_weight_ref, new_gain_ref, ready_ref, sent_sem, part_ref, part_sem, held_ref, held_sem = refs[-8:]
    tall, chunk = 16, ROWS // SEGMENTS

    def rows_of(segment):
        return pl.ds(segment * chunk, chunk)

    def code_of(segment):
        if len(code_refs) == 1 or segment * chunk < AHEAD:
            return code_refs[0].at[rows_of(segment)]
        return code_refs[1].at[pl.ds(segment * chunk - AHEAD, chunk)]

    def rows_at(index, carry):
        here = pl.ds(pl.multiple_of(index * tall, tall), tall)
        far_half = held_ref[here, :].astype(jnp.int32).astype(jnp.float32) * side_ref[:, :HQ]
        ready_ref[here, :] = part_ref[here, :] + far_half
        return carry

    arriving, leaving = [], []
    for segment in range(SEGMENTS):
        rows = rows_of(segment)
        arriving.append(pltpu.make_async_copy(part_weight_ref.at[rows], part_ref.at[rows], part_sem.at[segment]))
        arriving.append(pltpu.make_async_copy(code_of(segment), held_ref.at[rows], held_sem.at[segment]))
        leaving.append(pltpu.make_async_copy(ready_ref.at[rows], new_weight_ref.at[rows], sent_sem.at[segment]))
    for copy in arriving:
        copy.start()
    for segment in range(SEGMENTS):
        arriving[2 * segment].wait()
        arriving[2 * segment + 1].wait()
        lax.fori_loop(segment * chunk // tall, (segment + 1) * chunk // tall, rows_at, 0)
        leaving[segment].start()
    new_gain_ref[...] = part_gain_ref[...] + side_ref[:, HQ:] * 0.5
    for copy in leaving:
        copy.wait()


def mix(part_weight, part_gain, side, codes):
    vmem, anywhere = pl.BlockSpec(memory_space=pltpu.VMEM), pl.BlockSpec(memory_space=pl.ANY)
    return call(
        mix_kernel,
        (0, 0),
        PART_VMEM,
        in_specs=[anywhere, vmem, vmem] + [anywhere] * len(codes),
        out_specs=[anywhere, vmem],
        out_shape=[
            jax.ShapeDtypeStruct((ROWS, HQ), jnp.float32),
            jax.ShapeDtypeStruct((1, ROWS), jnp.float32),
        ],
        scratch_shapes=[
            pltpu.VMEM((ROWS, HQ), jnp.float32),
            pltpu.SemaphoreType.DMA((SEGMENTS,)),
            pltpu.VMEM((ROWS, HQ), jnp.float32),
            pltpu.SemaphoreType.DMA((SEGMENTS,)),
            pltpu.VMEM((ROWS, HQ), jnp.int16),
            pltpu.SemaphoreType.DMA((SEGMENTS,)),
        ],
    )(part_weight, part_gain, side, *codes)


def travel(block, target):
    sizes = (REP, NX, NY, NC)
    route = []
    for source in range(REP * NX * NY * NC):
        rep, rest = divmod(source, NX * NY * NC)
        x, rest = divmod(rest, NY * NC)
        y, core = divmod(rest, NC)
        place = 0
        for index, size in zip(target(rep, x, y, core), sizes):
            place = place * size + index % size
        route.append((source, place))
    return lax.ppermute(block, AXES, route)


def along_x(block, hop):
    return travel(block, lambda rep, x, y, core: (rep, x + hop, y, core))


def along_rep(block, hop):
    return travel(block, lambda rep, x, y, core: (rep + hop, x, y, core))


def two_ahead_backwards(block):
    def first(rep, x, y, core):
        return rep // 8 * 8 + (rep % 8 - 3) % 8, x, y, core

    def second(rep, x, y, core):
        passes = (rep % 8 + 3) % 8 >= 6
        return (rep // 8 + passes) % 2 * 8 + (rep % 8 - 3) % 8, x, y, core

    return travel(travel(block, first), second)


def other_y(block):
    return travel(block, lambda rep, x, y, core: (rep, x, 1 - y, core))


def other_core(block):
    return travel(block, lambda rep, x, y, core: (rep, x, y, 1 - core))


def finish(sent, order, columns, parts, hats, weight, weight_m, weight_v, column, gain, gain_m, gain_v, partner):
    far = other_core(sent)
    own = product(order, columns, parts, False)
    return tuple(update(hats, own, far, weight, weight_m, weight_v, column, gain, gain_m, gain_v, partner))


def nothing(*given):
    return jnp.zeros((ROWS, HQ), jnp.float32), jnp.zeros((1, ROWS), jnp.float32)


def exchange(
    step, code, head, tail, side, scaled, across, left, right, turned, order, own_order, hats, weight, weight_m, weight_v,
    column, gain, gain_m, gain_v, distance,
):
    if distance == 2:
        codes = along_rep(head, 2), two_ahead_backwards(tail)
    else:
        codes = (along_rep(code, distance),)
    far_side = along_rep(side, distance)
    right_across, beyond = along_x(across, -1), along_x(left, 1)
    columns = lax.all_to_all(turned, ("x", "y"), split_axis=0, concat_axis=0, tiled=True)
    left_across = along_x(across, 1)
    right_across, beyond = lax.optimization_barrier((right_across, beyond))
    parts = scaled, across, left, right, right_across, beyond, left_across, along_x(right_across, -1)
    apart = distance in (2, 4)
    ended = lax.cond(
        step > 0, finish, nothing, product(order, columns, parts, True), own_order, columns, parts, hats,
        weight, weight_m, weight_v, column, gain, gain_m, gain_v, () if apart else (*codes, far_side),
    )
    return tuple(mix(*ended, far_side, codes)) if apart else ended


def shards(step_index, tokens, cotangent, weight, weight_m, weight_v, gain, gain_m, gain_v):
    step = step_index[0]
    step_float = step.astype(jnp.float32)
    hats = 1.0 / (1.0 - jnp.power(jnp.array([BETA_ONE, BETA_TWO], jnp.float32), step_float))
    x, y, core = lax.axis_index("x"), lax.axis_index("y"), lax.axis_index("core")
    near = ((0, y), (0, 1 - y), (-1, y), (1, y), (1, 1 - y), (2, y), (-1, 1 - y), (2, 1 - y))
    places = [(x + hop) % NX * NY + lane for hop, lane in near]
    orders = [jnp.stack([*places, which]).astype(jnp.int32) for which in (1 - core, core)]

    scaled = scale_cotangent(tokens[0], cotangent[0])
    across, left, right = other_y(scaled), along_x(scaled, 1), along_x(scaled, -1)
    code, head, tail, scale, column = code_weight(weight[0], gain)
    turned = turn_tokens(tokens[0])
    side = jnp.concatenate([scale, gain], axis=1)
    side, hats, order, own_order = lax.optimization_barrier((side, hats, *orders))
    levels = REP.bit_length() - 1
    branches = [partial(exchange, distance=2**bit) for bit in range(levels)]
    new_weight, new_gain = lax.switch(
        step % levels, branches, step, code, head, tail, side, scaled, across, left, right, turned, order, own_order, hats,
        weight[0], weight_m[0], weight_v[0], column, gain, gain_m, gain_v,
    )
    return new_weight[None], new_gain


def solution(mesh):
    inner = Mesh(mesh.devices.reshape(REP, NX, NY, NC), AXES)
    fsdp = ("x", "y", "core")
    tall, thin = P("rep", fsdp, None), P("rep", fsdp)
    in_specs = (P(), tall, tall, tall, tall, tall, thin, thin, thin)
    return jax.shard_map(shards, mesh=inner, in_specs=in_specs, out_specs=(tall, thin), check_vma=False)
```
